256 devices in a mesh: hist: 64 (over z, y, core), mp: 4 (over x).
Axes of the slice: x: 4, y: 4, z: 8, core: 2. Of those that a mesh axis runs over, the one named last changes fastest.
Arguments:
- candidates: bfloat16 [65536, 1024], P('hist'), may hold values from -6 to 6
- w_gate: bfloat16 [1024, 1024], P(None, 'mp'), may hold values from -0.1875 to 0.1875
- w_query: bfloat16 [1024, 1024], P(None, 'mp'), may hold values from -0.1875 to 0.1875
- w_out: bfloat16 [1024, 1024], replicated, may hold values from -0.1875 to 0.1875
- gain: float32 [1024], P('mp'), may hold values from 0.1 to 1.9
- key_cache: bfloat16 [128, 3072, 1024], P('hist', None, 'mp'), may hold values from -6 to 6
- value_cache: bfloat16 [128, 3072, 1024], P('hist', None, 'mp'), may hold values from -6 to 6
- hist_blocks: int32 [128], P('hist'), may hold values from 12 to 24
- request_owner: int32 [4096, 1], P('hist'), may hold values from 0 to 63; in each aligned block of 64 rows (0 to 63, 64 to 127, ...) at most 2 rows name the same one
- request_slot: int32 [4096], P('hist'), may hold values from 0 to 1
- block_offsets: int32 [4096, 12], P('hist'), may hold values from 0 to 11
Outputs:
- scored: bfloat16 [65536, 1024], P('hist', 'mp')
The draws below stay inside these ranges and needn't reach their ends.
Inputs may be any that keep to these rules, and one draw needn't show every extreme that they name: `request_owner`: among the 64 requests of one index of hist, at most 2 name the same owner, a bound that some block reaches.
All inputs are finite; a program needn't handle non-finite values.
Results may differ from the reference program's by a relative error of at most 0.007.
Values may be sent and summed in bfloat16 or wider, within the bound.
A program may use at most 64 MiB of HBM per device.

```python
import math
import jax
import jax.numpy as jnp
import numpy as np
from jax import lax

D = 1024
H = 8
DH = 128
HD = 1024
CAND = 16
REQ_DEV = 64
REQUESTS = 4096
CAP = 2
USERS_DEV = 2
USERS = 128
BLK = 128
HBLK = 24
NSEL = 12
N_HIST = 64


def with_ends(values, key, low, high):
    longest = values.shape.index(max(values.shape))
    spots = []
    for shift in (0, 1):
        where = [jax.random.randint(jax.random.fold_in(key, axis), (), 0, length) for axis, length in enumerate(values.shape)]
        where[longest] = (where[longest] + shift) % values.shape[longest]
        spots.append(tuple(where))
    return values.at[spots[0]].set(low).at[spots[1]].set(high)


def steps_of(key, extent, pieces, smallest, top_value):
    def one(axis_at, shards_of):
        draws = jax.random.uniform(jax.random.fold_in(jax.random.fold_in(key, 6), axis_at), (shards_of,), jnp.float32, smallest / len(pieces), top_value / len(pieces))
        return jnp.repeat(jnp.exp(draws), extent[axis_at] // shards_of).reshape((-1,) + (1,) * (len(extent) - axis_at - 1))

    level = one(*pieces[0])
    for cut in pieces[1:]:
        level = level * one(*cut)
    return level


def assign_block(own_key, own, number, rows, number_of, top, reach, skew):
    sequence = jax.random.permutation(own_key, number_of)
    crowded, common = shares(number_of, rows * top, reach, skew, True), shares(number_of, rows * top, reach, skew, False)
    places = jnp.arange(number_of)

    def named(sizes, rotation):
        used = int((sizes > 0).sum())
        fixed = max(1, used // 4)
        shifted = fixed + (places - fixed + rotation * (used - fixed)) % max(1, number_of - fixed)
        return jnp.zeros((number_of,), jnp.int32).at[sequence[jnp.where(places < fixed, places, shifted)]].set(jnp.asarray(sizes, jnp.int32))

    sizes = jnp.where(number % 4 == 0, named(crowded, number // 4), named(common, number - number // 4 - 1))
    mixed = jax.random.permutation(jax.random.fold_in(own, 3), number_of)
    source_of, taker = mixed[0:number_of // 2 * 2:2], mixed[1:number_of // 2 * 2:2]
    margin = jnp.minimum(sizes[source_of] - 1, reach - sizes[taker]) // 2
    margin = jnp.where((source_of == sequence[0]) | (taker == sequence[0]) | (sizes[taker] == 0), 0, jnp.maximum(margin, 0))
    shifted = jax.random.randint(jax.random.fold_in(own, 4), (number_of // 2,), 0, 1 << 20) % (margin + 1)
    sizes = sizes.at[source_of].add(-shifted).at[taker].add(shifted)
    labels = jnp.searchsorted(jnp.cumsum(sizes), jnp.arange(rows * top), side="right").astype(jnp.int32)
    grid = labels.reshape(top, rows).T
    grid = grid[jax.random.permutation(jax.random.fold_in(own, 1), rows)]
    rotation = jax.random.randint(jax.random.fold_in(own, 2), (rows, 1), 0, top)
    return jnp.take_along_axis(grid, (jnp.arange(top)[None, :] + rotation) % top, axis=1)


def shares(count, total, reach, skew, full):
    loads = [(1 << 20) // math.isqrt(rank ** skew) + 1 for rank in range(1, count + 1)]
    largest = reach if full else min(reach, max(-(-total // count), total * loads[0] // sum(loads)))
    least = 1 if total - largest >= count - 1 else 0
    holding, rest = [largest] + [least] * (count - 1), total - largest - least * (count - 1)
    while rest > 0:
        movable = [i for i in range(1, count) if holding[i] < largest] or [i for i in range(1, count) if holding[i] < reach]
        mass, left = sum([loads[i] for i in movable]), rest
        for i in movable:
            addition = min(reach - holding[i], max(1, left * loads[i] // mass), rest)
            holding[i] = holding[i] + addition
            rest = rest - addition
    return np.array(holding)


def bell_draw(own_key, shape, spread, most, shards=(), held_as=jnp.bfloat16):
    level = steps_of(own_key, shape, shards, -0.22, 0.18) if shards else 1.0
    values = jax.random.normal(own_key, shape, jnp.float32) * spread * level
    return jnp.minimum(jnp.maximum(values, -most), most).astype(held_as)


def setup_inputs(seed: int = 0) -> dict:
    key_of = jax.random.split(jax.random.key(seed), 12)
    candidates = bell_draw(key_of[0], (REQUESTS * CAND, D), 1.0, 6.0, ((0, 64),))
    w_gate = bell_draw(key_of[1], (D, HD), D ** -0.5, 0.1875, ((1, 4),))
    w_query = bell_draw(key_of[2], (D, HD), D ** -0.5, 0.1875, ((1, 4),))
    w_out = bell_draw(key_of[3], (HD, D), HD ** -0.5, 0.1875)
    gain = jnp.clip(1.0 + 0.18 * jax.random.normal(key_of[4], (HD,), jnp.float32), 0.1, 1.9)
    key_cache = bell_draw(key_of[5], (USERS, HBLK * BLK, HD), 1.0, 6.0, ((0, 64), (2, 4)))
    value_cache = bell_draw(key_of[6], (USERS, HBLK * BLK, HD), 1.0, 6.0, ((0, 64), (2, 4)))
    hist_blocks = with_ends(jax.random.randint(key_of[7], (USERS,), HBLK // 2, HBLK + 1), jax.random.fold_in(key_of[7], 1), HBLK // 2, HBLK).astype(jnp.int32)
    request_owner_keys = jax.random.split(jax.random.fold_in(key_of[8], 1), REQUESTS // REQ_DEV)
    request_owner_turns = jax.random.permutation(jax.random.fold_in(key_of[8], 3), REQUESTS // REQ_DEV)
    request_owner = jax.vmap(lambda own, number: assign_block(jax.random.fold_in(key_of[8], 2), own, number, REQ_DEV, N_HIST, 1, CAP, 2))(request_owner_keys, request_owner_turns).reshape((REQUESTS, 1))
    request_slot = with_ends(jax.random.randint(key_of[9], (REQUESTS,), 0, USERS_DEV), jax.random.fold_in(key_of[9], 1), 0, USERS_DEV - 1).astype(jnp.int32)
    block_offsets = with_ends(jax.random.randint(key_of[10], (REQUESTS, NSEL), 0, HBLK // 2), jax.random.fold_in(key_of[10], 1), 0, (HBLK // 2) - 1).astype(jnp.int32)
    return dict(candidates=candidates, w_gate=w_gate, w_query=w_query, w_out=w_out, gain=gain, key_cache=key_cache, value_cache=value_cache, hist_blocks=hist_blocks, request_owner=request_owner, request_slot=request_slot, block_offsets=block_offsets)


def reference(candidates, w_gate, w_query, w_out, gain, key_cache, value_cache, hist_blocks, request_owner, request_slot, block_offsets):
    gate_u = jax.nn.silu(jnp.dot(candidates, w_gate, preferred_element_type=jnp.float32))
    query = jax.nn.silu(jnp.dot(candidates, w_query, preferred_element_type=jnp.float32)).astype(jnp.bfloat16)
    users = (request_owner[:, 0] * USERS_DEV + request_slot).astype(jnp.int32)
    picked = (hist_blocks[users][:, None] - 1 - block_offsets).astype(jnp.int32)
    block_rows = (users[:, None] * HBLK + picked).astype(jnp.int32)
    key_blocks = key_cache.reshape(USERS * HBLK, BLK, HD)
    value_blocks = value_cache.reshape(USERS * HBLK, BLK, HD)
    group = math.gcd(REQUESTS, 16)
    queries = query.reshape(REQUESTS // group, group, CAND, H, DH)
    rows_grouped = block_rows.reshape(REQUESTS // group, group, NSEL)
    scale = DH ** (-0.5)

    def attend_group(pair):
        query_group, row_group = pair
        keys = key_blocks[row_group].reshape(group, NSEL * BLK, H, DH).astype(jnp.float32)
        values = value_blocks[row_group].reshape(group, NSEL * BLK, H, DH).astype(jnp.float32)
        scores = jnp.einsum('gchd,gkhd->ghck', query_group.astype(jnp.float32), keys) * scale
        weights = jax.nn.silu(scores).astype(jnp.bfloat16)
        weights = lax.optimization_barrier(weights).astype(jnp.float32)
        result = jnp.einsum('ghck,gkhd->gchd', weights, values)
        return result.astype(jnp.bfloat16)
    attended = lax.map(attend_group, (queries, rows_grouped)).reshape(REQUESTS * CAND, HD)
    widened = attended.astype(jnp.float32)
    mean = lax.optimization_barrier(jnp.sum(widened, axis=-1)) / HD
    var = lax.optimization_barrier(jnp.sum(widened * widened, axis=-1)) / HD - mean * mean
    normed = (widened - mean[:, None]) / jnp.sqrt(var[:, None] + 1e-05)
    gated = (normed * gain[None, :] * gate_u).astype(jnp.bfloat16)
    total = jnp.dot(gated, w_out, preferred_element_type=jnp.float32) + candidates.astype(jnp.float32)
    return total.astype(jnp.bfloat16)
```

```python
import jax
import jax.numpy as jnp
from jax import lax
from jax.experimental import pallas as pl
from jax.experimental.pallas import tpu as pltpu
from jax.sharding import PartitionSpec as P

MESH = pl.DeviceIdType.MESH
F32 = jnp.float32
BF16 = jnp.bfloat16

NZ, NY, NC = 8, 4, 2
NH = NZ * NY * NC
CHUNKS, PER = 8, 8
NX = 4
CAP = 2
CAND = 16
REQ = 64
DH = 128
WIN = 12
HBLK = 24
SUB = CAND // NX
ROWS = PER * CAP * CAND
GRP = 4


def step_shift(k):
    chunk, dz = lax.div(k, PER), lax.rem(k, PER)
    low = lax.rem(chunk + dz, PER)
    return dz, lax.div(low, NC), lax.rem(low, NC)


def peer_of(h, k, sign):
    z, y, c = lax.div(h, NY * NC), lax.rem(lax.div(h, NC), NY), lax.rem(h, NC)
    dz, dy, dc = step_shift(k)
    z = lax.rem(z + NZ + sign * dz, NZ)
    y = lax.rem(y + NY + sign * dy, NY)
    c = lax.rem(c + dc, NC)
    return (z * NY + y) * NC + c


def silu(v):
    half = v * 0.5
    return half + half * jnp.tanh(half)


def kernel(
    idx_ref,
    hb_ref,
    mrow_ref,
    tgt_ref,
    gain_ref,
    cand_hbm,
    wq_hbm,
    wg_hbm,
    wo_hbm,
    k_hbm,
    v_hbm,
    out_ref,
    cand_v,
    wq_v,
    wg_v,
    wo_v,
    k_v,
    v_v,
    q_v,
    sendq,
    sendm,
    recvq,
    recvm,
    mexp,
    xs,
    xr,
    ans,
    perm,
    place,
    csub,
    gg,
    gains,
    att,
    outs,
    load_sem,
    fq_send,
    fm_send,
    fq_recv,
    fm_recv,
    w_send,
    w_recv,
    g_send,
    g_recv,
    x_send,
    x_recv,
    a_send,
    a_recv,
    o_send,
    o_recv,
    o_own,
):
    h = lax.axis_index("hist")
    me = lax.axis_index("mp")

    barrier = pltpu.get_barrier_semaphore()

    def greet(k, carry):
        pl.semaphore_signal(
            barrier, inc=1, device_id=(peer_of(h, k, 1), me), device_id_type=MESH
        )
        return carry

    loads = [
        pltpu.make_async_copy(cand_hbm, cand_v, load_sem.at[0]),
        pltpu.make_async_copy(wq_hbm, wq_v, load_sem.at[1]),
        pltpu.make_async_copy(wg_hbm, wg_v.at[me], load_sem.at[2]),
        pltpu.make_async_copy(k_hbm, k_v, load_sem.at[3]),
        pltpu.make_async_copy(v_hbm, v_v, load_sem.at[4]),
    ] + [
        pltpu.make_async_copy(
            wo_hbm.at[:, pl.ds(b * 256, 256)], wo_v.at[b], load_sem.at[5 + b]
        )
        for b in range(NX)
    ]
    for load in loads:
        load.start()
    lax.fori_loop(1, NH, greet, 0)
    for d in range(1, NX):
        pl.semaphore_signal(
            barrier, inc=1, device_id=(h, lax.rem(me + d, NX)), device_id_type=MESH
        )

    loads[0].wait()
    loads[1].wait()

    def project(t, carry):
        acc = jnp.dot(
            cand_v[pl.ds(pl.multiple_of(t * 256, 256), 256), :],
            wq_v[...],
            preferred_element_type=F32,
        )
        q_v[pl.ds(t * 16, 16)] = silu(acc).astype(BF16).reshape(16, CAND, 2 * DH)
        return carry

    lax.fori_loop(0, 4, project, 0)

    pl.semaphore_wait(barrier, NH - 1 + NX - 1)

    def fq_copy(k):
        return pltpu.make_async_remote_copy(
            src_ref=sendq.at[k],
            dst_ref=recvq.at[k],
            send_sem=fq_send,
            recv_sem=fq_recv.at[lax.div(k, PER)],
            device_id=(peer_of(h, k, 1), me),
            device_id_type=MESH,
        )

    def fm_copy(k):
        return pltpu.make_async_remote_copy(
            src_ref=sendm.at[k],
            dst_ref=recvm.at[k],
            send_sem=fm_send,
            recv_sem=fm_recv.at[lax.div(k, PER)],
            device_id=(peer_of(h, k, 1), me),
            device_id_type=MESH,
        )

    for c in range(CAP):
        r = idx_ref[c]
        recvq[0, pl.ds(c * CAND, CAND), :] = q_v[r]
        recvm[0, pl.ds(c, 1), :] = mrow_ref[r]

    def forward(k, carry):
        for c in range(CAP):
            r = idx_ref[k * CAP + c]
            sendq[k, pl.ds(c * CAND, CAND), :] = q_v[r]
            sendm[k, pl.ds(c, 1), :] = mrow_ref[r]
        fm_copy(k).start()
        fq_copy(k).start()
        return carry

    lax.fori_loop(1, NH, forward, 0)

    loads[2].wait()

    def w_copy(d):
        return pltpu.make_async_remote_copy(
            src_ref=wg_v.at[me],
            dst_ref=wg_v.at[me],
            send_sem=w_send.at[d - 1],
            recv_sem=w_recv.at[d - 1],
            device_id=(h, lax.rem(me + d, NX)),
            device_id_type=MESH,
        )

    def g_copy(d):
        return pltpu.make_async_remote_copy(
            src_ref=gain_ref,
            dst_ref=gains.at[me],
            send_sem=g_send.at[d - 1],
            recv_sem=g_recv.at[d - 1],
            device_id=(h, lax.rem(me + d, NX)),
            device_id_type=MESH,
        )

    for d in (2, 1, 3):
        g_copy(d).start()
        w_copy(d).start()
    gains[me] = gain_ref[...]

    def one_hot(t, carry):
        rows = pl.ds(pl.multiple_of(t * 128, 128), 128)
        i = lax.broadcasted_iota(jnp.int32, (128, 512), 0) + t * 128
        col = lax.broadcasted_iota(jnp.int32, (128, 512), 1)
        j, src, head = i >> 7, (i >> 4) & 7, (i >> 3) & 1
        slot, c = (i >> 2) & 1, i & 3
        want = head * 256 + src * 32 + slot * 16 + j * 4 + c
        perm[rows, :] = jnp.where(col == want, 1.0, 0.0).astype(BF16)
        return carry

    lax.fori_loop(0, 4, one_hot, 0)

    def placing(t, carry):
        rows = pl.ds(pl.multiple_of(t * 64, 64), 64)
        want = tgt_ref[rows, :]
        col = lax.broadcasted_iota(jnp.int32, (64, 1024), 1)
        for head in range(2):
            place[head, rows, :] = jnp.where(col == want + head * 8, 1.0, 0.0).astype(BF16)
        i = lax.broadcasted_iota(jnp.int32, (64, 1024), 0) + t * 64
        mine = (i >> 2) * 16 + me * SUB + (i & 3)
        pick = jnp.where(col == mine, 1.0, 0.0).astype(BF16)
        for b in range(NX):
            csub[b, rows, :] = jnp.dot(
                pick, cand_v[:, b * 256 : (b + 1) * 256], preferred_element_type=F32
            ).astype(BF16)
        return carry

    lax.fori_loop(0, 4, placing, 0)

    loads[3].wait()
    loads[4].wait()

    def x_copy(i, d):
        there = lax.rem(me + d, NX)
        return pltpu.make_async_remote_copy(
            src_ref=xs.at[i, there],
            dst_ref=xr.at[i, :, me],
            send_sem=x_send.at[d - 1],
            recv_sem=x_recv.at[i, d - 1],
            device_id=(h, there),
            device_id_type=MESH,
        )

    def a_copy(i, s):
        k = i * PER + s
        return pltpu.make_async_remote_copy(
            src_ref=xr.at[i, s],
            dst_ref=ans.at[k],
            send_sem=a_send,
            recv_sem=a_recv.at[i],
            device_id=(peer_of(h, k, -1), me),
            device_id_type=MESH,
        )

    def give_back(i):
        for d in range(1, NX):
            x_copy(i, d).wait_recv()

        def one(s, carry):
            a_copy(i, s).start()
            return carry

        @pl.when(i == 0)
        def _():
            ans[0] = xr[0, 0]
            lax.fori_loop(1, PER, one, 0)

        @pl.when(i > 0)
        def _():
            lax.fori_loop(0, PER, one, 0)

    def wait_chunk(buf, sem, i):
        @pl.when(i == 0)
        def _():
            part = buf.at[pl.ds(1, PER - 1)]
            pltpu.make_async_copy(part, part, sem.at[0]).wait()

        @pl.when(i > 0)
        def _():
            part = buf.at[pl.ds(i * PER, PER)]
            pltpu.make_async_copy(part, part, sem.at[i]).wait()

    half_scale = 0.5 * DH ** (-0.5)

    def attend(i, carry):
        wait_chunk(recvm, fm_recv, i)
        wait_chunk(recvq, fq_recv, i)
        for s in range(PER):
            for c in range(CAP):
                mexp[pl.ds((s * CAP + c) * CAND, CAND), :] = jnp.broadcast_to(
                    recvm[i * PER + s, pl.ds(c, 1), :], (CAND, 128)
                )
        q = recvq[pl.ds(i * PER, PER)].reshape(ROWS, 2 * DH)
        done = []
        for head in range(2):
            lanes = slice(head * DH, (head + 1) * DH)
            qh = q[:, lanes]
            total = None
            for u in range(2):
                for g in range(WIN // GRP):
                    first = u * HBLK + jnp.maximum(hb_ref[u] - WIN, 0) + g * GRP
                    keys = k_v[pl.ds(first, GRP), :, lanes].reshape(GRP * 128, DH)
                    vals = v_v[pl.ds(first, GRP), :, lanes].reshape(GRP * 128, DH)
                    s = lax.dot_general(
                        qh, keys, (((1,), (1,)), ((), ())), preferred_element_type=F32
                    )
                    parts = []
                    for b in range(GRP):
                        lane = u * WIN + g * GRP + b
                        v = s[:, b * 128 : (b + 1) * 128] * half_scale
                        w = (v + v * jnp.tanh(v)) * mexp[:, lane : lane + 1]
                        parts.append(w.astype(BF16))
                    w = jnp.concatenate(parts, axis=1)
                    r = jnp.dot(w, vals, preferred_element_type=F32)
                    total = r if total is None else total + r
            done.append(total.astype(BF16))
        stacked = jnp.concatenate(done, axis=0)
        moved = jnp.dot(perm[...], stacked, preferred_element_type=F32).astype(BF16)
        xs[i] = moved.reshape(NX, PER, CAND, DH)
        for d in (2, 1, 3):
            x_copy(i, d).start()
        xr[i, :, me] = xs[i, me]

        @pl.when(i > 0)
        def _():
            give_back(i - 1)

        return carry

    lax.fori_loop(0, CHUNKS, attend, 0)
    give_back(jnp.int32(CHUNKS - 1))

    for d in range(1, NX):
        w_copy(d).wait_recv()
        g_copy(d).wait_recv()

    def gate(b, carry):
        acc = jnp.zeros((256, 256), F32)
        for c in range(NX):
            acc += jnp.dot(
                csub[c], wg_v[b, c * 256 : (c + 1) * 256, :], preferred_element_type=F32
            )
        gg[b] = silu(acc) * gains[b]
        return carry

    lax.fori_loop(0, NX, gate, 0)
    for load in loads[5:]:
        load.wait()

    lax.fori_loop(0, CHUNKS, lambda i, c: (wait_chunk(ans, a_recv, i), c)[1], 0)

    for pair in range(2):
        rows = jnp.concatenate(
            [ans[:, 2 * pair + t].reshape(NH * CAND, DH) for t in range(2)], axis=1
        )
        for head in range(2):
            r = jnp.dot(place[head], rows, preferred_element_type=F32)
            for t in range(2):
                lo = ((2 * pair + t) * 2 + head) * DH
                att[:, lo : lo + DH] = r[:, t * DH : (t + 1) * DH]
    full = att[...]
    mean = jnp.sum(full, axis=-1, keepdims=True) * (1.0 / 1024)
    var = jnp.sum(full * full, axis=-1, keepdims=True) * (1.0 / 1024) - mean * mean
    rstd = 1.0 / jnp.sqrt(var + 1e-5)
    gated = [
        ((att[:, b * 256 : (b + 1) * 256] - mean) * rstd * gg[b]).astype(BF16)
        for b in range(NX)
    ]

    def o_copy(d):
        there = lax.rem(me + d, NX)
        return pltpu.make_async_remote_copy(
            src_ref=outs.at[there],
            dst_ref=out_ref.at[me],
            send_sem=o_send.at[d - 1],
            recv_sem=o_recv.at[d - 1],
            device_id=(h, there),
            device_id_type=MESH,
        )

    for d in (2, 1, 3, 0):
        there = lax.rem(me + d, NX)
        acc = csub[there].astype(F32)
        for b in range(NX):
            acc += jnp.dot(
                gated[b],
                wo_v[there, b * 256 : (b + 1) * 256, :],
                preferred_element_type=F32,
            )
        outs[there] = acc.astype(BF16)
        if d:
            o_copy(d).start()
    own = pltpu.make_async_copy(outs.at[me], out_ref.at[me], o_own)
    own.start()

    part = sendq.at[pl.ds(1, NH - 1)]
    pltpu.make_async_copy(part, part, fq_send).wait()
    part = sendm.at[pl.ds(1, NH - 1)]
    pltpu.make_async_copy(part, part, fm_send).wait()
    part = ans.at[pl.ds(1, NH - 1)]
    pltpu.make_async_copy(part, part, a_send).wait()
    for d in range(1, NX):
        part = xs.at[:, 0]
        pltpu.make_async_copy(part, part, x_send.at[d - 1]).wait()
        w_copy(d).wait_send()
        g_copy(d).wait_send()
    own.wait()
    for d in range(1, NX):
        o_copy(d).wait()


def on_device(
    candidates,
    w_gate,
    w_query,
    w_out,
    gain,
    key_cache,
    value_cache,
    hist_blocks,
    request_owner,
    request_slot,
    block_offsets,
):
    h = lax.axis_index("hist")
    owners = request_owner[:, 0]
    order = jnp.arange(REQ, dtype=jnp.int32)
    same_owner = owners[None, :] == owners[:, None]
    earlier = order[None, :] < order[:, None]
    rank = jnp.sum(jnp.where(same_owner & earlier, 1, 0), axis=1).astype(jnp.int32)
    dz = (owners // (NY * NC) - h // (NY * NC)) % NZ
    dy = (owners // NC % NY - h // NC % NY) % NY
    dc = (owners % NC + h % NC) % NC
    step = (dy * NC + dc - dz) % PER * PER + dz
    place = step * CAP + rank
    slots = jnp.arange(NH * CAP, dtype=jnp.int32)
    idx = jnp.sum(jnp.where(slots[:, None] == place[None, :], order[None, :], 0), axis=1)
    lane = request_slot[:, None] * WIN + WIN - 1 - block_offsets
    mrow = jnp.sum(
        jnp.where(lane[:, :, None] == jnp.arange(128, dtype=jnp.int32), 1.0, 0.0), axis=1
    ).reshape(REQ, 1, 128)
    tgt = (step * 16 + rank * SUB)[:, None] + jnp.arange(SUB, dtype=jnp.int32)
    tgt = tgt.reshape(REQ * SUB, 1)

    vmem = pl.BlockSpec(memory_space=pltpu.VMEM)
    smem = pl.BlockSpec(memory_space=pltpu.SMEM)
    anyw = pl.BlockSpec(memory_space=pl.ANY)
    dma = pltpu.SemaphoreType.DMA
    out = pl.pallas_call(
        kernel,
        out_shape=jax.ShapeDtypeStruct((NX, REQ * SUB, 256), BF16),
        in_specs=[smem, smem, vmem, vmem, vmem] + [anyw] * 6,
        out_specs=anyw,
        scratch_shapes=[
            pltpu.VMEM((1024, 1024), BF16),
            pltpu.VMEM((1024, 256), BF16),
            pltpu.VMEM((NX, 1024, 256), BF16),
            pltpu.VMEM((NX, 1024, 256), BF16),
            pltpu.VMEM((2 * HBLK, 128, 256), BF16),
            pltpu.VMEM((2 * HBLK, 128, 256), BF16),
            pltpu.VMEM((REQ, CAND, 256), BF16),
            pltpu.VMEM((NH, CAP * CAND, 256), BF16),
            pltpu.VMEM((NH, CAP, 128), F32),
            pltpu.VMEM((NH, CAP * CAND, 256), BF16),
            pltpu.VMEM((NH, CAP, 128), F32),
            pltpu.VMEM((ROWS, 128), F32),
            pltpu.VMEM((CHUNKS, NX, PER, CAND, DH), BF16),
            pltpu.VMEM((CHUNKS, PER, NX, CAND, DH), BF16),
            pltpu.VMEM((NH, NX, CAND, DH), BF16),
            pltpu.VMEM((512, 512), BF16),
            pltpu.VMEM((2, 256, 1024), BF16),
            pltpu.VMEM((NX, 256, 256), BF16),
            pltpu.VMEM((NX, 256, 256), F32),
            pltpu.VMEM((NX, 1, 256), F32),
            pltpu.VMEM((256, 1024), F32),
            pltpu.VMEM((NX, 256, 256), BF16),
            dma((9,)),
            dma,
            dma,
            dma((CHUNKS,)),
            dma((CHUNKS,)),
            dma((3,)),
            dma((3,)),
            dma((3,)),
            dma((3,)),
            dma((3,)),
            dma((CHUNKS, 3)),
            dma,
            dma((CHUNKS,)),
            dma((3,)),
            dma((3,)),
            dma,
        ],
        compiler_params=pltpu.CompilerParams(
            collective_id=0, has_side_effects=True, vmem_limit_bytes=56 * 1024 * 1024
        ),
        name="attend_remote",
    )(
        idx,
        hist_blocks,
        mrow,
        tgt,
        gain.reshape(1, 256),
        candidates,
        w_query,
        w_gate,
        w_out,
        key_cache.reshape(2 * HBLK, 128, 256),
        value_cache.reshape(2 * HBLK, 128, 256),
    )
    return out.reshape(NX, REQ, SUB, 256).transpose(1, 0, 2, 3).reshape(REQ * CAND, 256)


def solution(mesh):
    in_specs = (
        P("hist", None),
        P(None, "mp"),
        P(None, "mp"),
        P(),
        P("mp"),
        P("hist", None, "mp"),
        P("hist", None, "mp"),
        P("hist"),
        P("hist", None),
        P("hist"),
        P("hist", None),
    )
    return jax.shard_map(
        on_device, mesh=mesh, in_specs=in_specs, out_specs=P("hist", "mp"), check_vma=False
    )
```

```python
import jax
import jax.numpy as jnp
from jax import lax
from jax.experimental import pallas as pl
from jax.experimental.pallas import tpu as pltpu
from jax.sharding import PartitionSpec as P

MESH = pl.DeviceIdType.MESH
F32 = jnp.float32
BF16 = jnp.bfloat16

NZ, NY, NC = 8, 4, 2
NH = NZ * NY * NC
CHUNKS, PER = 8, 8
NX = 4
CAP = 2
CAND = 16
REQ = 64
DH = 128
WIN = 12
HBLK = 24
SUB = CAND // NX
ROWS = PER * CAP * CAND
GRP = 4
UPFRONT = 8


def peer_of(h, low, dz, sign):
    z, y, c = h >> 3, (h >> 1) & 3, h & 1
    z = (z + sign * dz) & (NZ - 1)
    y = (y + sign * (low >> 1)) & (NY - 1)
    return z * (NY * NC) + y * NC + (c ^ (low & 1))


def silu(v):
    half = v * 0.5
    return half + half * jnp.tanh(half)


def kernel(
    hb_ref,
    own_ref,
    slot_ref,
    off_ref,
    gain_ref,
    cand_hbm,
    wq_hbm,
    wg_hbm,
    wo_hbm,
    k_hbm,
    v_hbm,
    out_ref,
    cand_v,
    wq_v,
    wg_v,
    wo_v,
    k_v,
    v_v,
    q_v,
    tcol,
    mall,
    sendq,
    sendm,
    recvq,
    recvm,
    mexp,
    xs,
    xr,
    ans,
    perm,
    place,
    csub,
    r4,
    gs,
    gr,
    att,
    outs,
    kt,
    load_sem,
    fq_send,
    fm_send,
    fq_recv,
    fm_recv,
    g_send,
    g_recv,
    x_send,
    x_recv,
    a_send,
    a_recv,
    o_send,
    o_recv,
    plane_sem,
    own_sem,
):
    h = lax.axis_index("hist")
    me = lax.axis_index("mp")

    barrier = pltpu.get_barrier_semaphore()

    def greet(sem, low, dz):
        pl.semaphore_signal(
            sem, inc=1, device_id=(peer_of(h, low, dz, 1), me), device_id_type=MESH
        )

    for d in range(1, PER):
        greet(barrier, 0, d)
    for d in range(1, NX):
        pl.semaphore_signal(
            barrier, inc=1, device_id=(h, lax.rem(me + d, NX)), device_id_type=MESH
        )
    for d in range(1, CHUNKS):
        greet(barrier, d, 0)

    loads = [
        pltpu.make_async_copy(cand_hbm, cand_v, load_sem.at[0]),
        pltpu.make_async_copy(wq_hbm, wq_v, load_sem.at[1]),
        pltpu.make_async_copy(wg_hbm, wg_v, load_sem.at[2]),
        pltpu.make_async_copy(k_hbm, k_v, load_sem.at[3]),
        pltpu.make_async_copy(v_hbm, v_v, load_sem.at[4]),
    ] + [
        pltpu.make_async_copy(
            wo_hbm.at[:, pl.ds(b * 256, 256)], wo_v.at[b], load_sem.at[5 + b]
        )
        for b in range(NX)
    ]
    for load in loads[:2]:
        load.start()

    def same_lanes(row, count):
        return jnp.broadcast_to(row, (count, REQ))

    def lanes_dot(a, b):
        return lax.dot_general(a, b, (((1,), (1,)), ((), ())), preferred_element_type=F32)

    def iota(shape, axis):
        return lax.broadcasted_iota(jnp.int32, shape, axis)

    def flag(hit):
        return jnp.where(hit, 1.0, 0.0)

    own = own_ref[...]
    own_f = own.astype(F32)
    eye = flag(iota((REQ, REQ), 0) == iota((REQ, REQ), 1)).astype(BF16)
    own_col = lanes_dot(eye, same_lanes(own_f, REQ).astype(BF16))
    twin = (own_col == same_lanes(own_f, REQ)) & (iota((REQ, REQ), 0) < iota((REQ, REQ), 1))
    rank = jnp.sum(flag(twin), axis=0, keepdims=True)
    low_own, low_h = own & (NY * NC - 1), lax.rem(h, NY * NC)
    dz = ((own >> 3) - lax.div(h, NY * NC) + NZ) & (NZ - 1)
    dy = ((low_own >> 1) - lax.div(low_h, NC) + NY) & (NY - 1)
    dc = (low_own + lax.rem(low_h, NC)) & (NC - 1)
    step = (dy * NC + dc) * PER + dz
    slot = (step * CAP).astype(F32) + rank
    slot_bf = same_lanes(slot, 128).astype(BF16)
    spread = flag(iota((REQ, 1024), 1) >> 4 == iota((REQ, 1024), 0)).astype(BF16)
    tcol[...] = jnp.dot(
        slot_bf[:8], spread, preferred_element_type=F32
    ) * CAND + (iota((8, 1024), 1) & (CAND - 1)).astype(F32)
    lane = slot_ref[...] * WIN + (WIN - 1)
    counts = jnp.zeros((32, REQ), F32)
    for j in range(WIN):
        counts += flag(same_lanes(lane - off_ref[pl.ds(j, 1), :], 32) == iota((32, REQ), 0))
    blank = jnp.zeros((32, REQ), F32)
    both = jnp.zeros((NH, 128), F32)
    for c in range(CAP):
        parts = [blank] * (2 * c) + [counts] + [blank] * (3 - 2 * c)
        mine = (iota((NH, REQ), 0) * CAP + c).astype(F32)
        held = flag(same_lanes(slot, NH) == mine).astype(BF16)
        both += lanes_dot(held, jnp.concatenate(parts, axis=0).astype(BF16))
    mall[...] = both

    loads[0].wait()
    loads[1].wait()
    for load in loads[2:]:
        load.start()

    def project(t, carry):
        rows = pl.ds(pl.multiple_of(t * 256, 256), 256)
        acc = jnp.dot(cand_v[rows, :], wq_v[...], preferred_element_type=F32)
        q_v[rows, :] = silu(acc).astype(BF16)
        return carry

    lax.fori_loop(0, 4, project, 0)

    pl.semaphore_wait(barrier, PER - 1 + CHUNKS - 1 + NX - 1)
    for d in range(1, CHUNKS):
        greet(plane_sem, d, 0)

    def fq_copy(i, dz):
        k = i * PER + dz
        return pltpu.make_async_remote_copy(
            src_ref=sendq.at[k],
            dst_ref=recvq.at[k],
            send_sem=fq_send,
            recv_sem=fq_recv.at[i],
            device_id=(peer_of(h, i, dz, 1), me),
            device_id_type=MESH,
        )

    def fm_copy(i, dz):
        k = i * PER + dz
        return pltpu.make_async_remote_copy(
            src_ref=sendm.at[k],
            dst_ref=recvm.at[k],
            send_sem=fm_send,
            recv_sem=fm_recv.at[i],
            device_id=(peer_of(h, i, dz, 1), me),
            device_id_type=MESH,
        )

    def forward(i, carry):
        row = (iota((ROWS, 1024), 0) + i * ROWS).astype(F32)
        pick = flag(row == jnp.broadcast_to(tcol[pl.ds(0, 1), :], (ROWS, 1024))).astype(BF16)
        got = jnp.dot(pick, q_v[...], preferred_element_type=F32).astype(BF16)
        sendq[pl.ds(i * PER, PER)] = got.reshape(PER, CAP * CAND, 2 * DH)

        def one(dz):
            k = i * PER + dz
            sendm[k] = mall[pl.ds(k, 1), :]
            fm_copy(i, dz).start()
            fq_copy(i, dz).start()

        @pl.when(i == 0)
        def _():
            recvq[0] = sendq[0]
            recvm[0] = mall[pl.ds(0, 1), :]

        @pl.when(i == 1)
        def _():
            pl.semaphore_wait(plane_sem, CHUNKS - 1)

        @pl.when(i > 0)
        def _():
            one(0)

        for dz in range(1, PER):
            one(dz)

        return carry

    lax.fori_loop(0, UPFRONT, forward, 0)

    def g_copy(d):
        there = lax.rem(me + d, NX)
        return pltpu.make_async_remote_copy(
            src_ref=gs.at[there],
            dst_ref=gr.at[me],
            send_sem=g_send.at[d - 1],
            recv_sem=g_recv.at[d - 1],
            device_id=(h, there),
            device_id_type=MESH,
        )

    i, col = iota((256, 256), 0), iota((256, 256), 1)
    r4[...] = flag(col == ((i >> 2) & 15) * 16 + (i >> 6) * 4 + (i & 3)).astype(BF16)

    loads[2].wait()

    def gate(t, carry):
        rows = pl.ds(pl.multiple_of(t * 256, 256), 256)
        part = pl.ds(pl.multiple_of(t * 64, 64), 64)
        acc = jnp.dot(cand_v[rows, :], wg_v[...], preferred_element_type=F32)
        g = (silu(acc) * gain_ref[...]).astype(BF16)
        moved = jnp.dot(r4[...], g, preferred_element_type=F32).astype(BF16)
        gs[:, part, :] = moved.reshape(NX, 64, 256)
        mine = r4[pl.ds(pl.multiple_of(me * 64, 64), 64), :]
        for b in range(NX):
            csub[b, part, :] = jnp.dot(
                mine, cand_v[rows, b * 256 : (b + 1) * 256], preferred_element_type=F32
            ).astype(BF16)
        return carry

    lax.fori_loop(0, 4, gate, 0)
    gr[me] = gs[me]

    def one_hot(t, carry):
        rows = pl.ds(pl.multiple_of(t * 128, 128), 128)
        i = lax.broadcasted_iota(jnp.int32, (128, 512), 0) + t * 128
        col = lax.broadcasted_iota(jnp.int32, (128, 512), 1)
        j, src, head = i >> 7, (i >> 4) & 7, (i >> 3) & 1
        slot, c = (i >> 2) & 1, i & 3
        want = head * 256 + src * 32 + slot * 16 + j * 4 + c
        perm[rows, :] = jnp.where(col == want, 1.0, 0.0).astype(BF16)
        return carry

    lax.fori_loop(0, 4, one_hot, 0)

    i = iota((256, REQ), 0)
    spread = flag(i >> 2 == iota((256, REQ), 1)).astype(BF16)
    want = lanes_dot(spread, slot_bf)
    c = iota((256, 128), 0) & 3
    for t in range(8):
        col = iota((256, 128), 1) + t * 128
        for head in range(2):
            sits = ((col >> 4) * 2 + ((col >> 2) & 1)).astype(F32)
            hit = (sits == want) & ((col & 3) == c) & (((col >> 3) & 1) == head)
            place[head, :, t * 128 : (t + 1) * 128] = flag(hit).astype(BF16)

    loads[3].wait()
    for b in range(WIN):
        for u in range(2):
            first = u * HBLK + jnp.maximum(hb_ref[u] - WIN, 0) + b
            for head in range(2):
                kt[u * 2 + head, :, b * 128 : (b + 1) * 128] = k_v[
                    first, :, head * DH : (head + 1) * DH
                ].T
    loads[4].wait()

    def x_copy(i, d):
        there = lax.rem(me + d, NX)
        return pltpu.make_async_remote_copy(
            src_ref=xs.at[i, there],
            dst_ref=xr.at[i, :, me],
            send_sem=x_send.at[d - 1],
            recv_sem=x_recv.at[i, d - 1],
            device_id=(h, there),
            device_id_type=MESH,
        )

    def a_copy(i, s):
        k = i * PER + s
        return pltpu.make_async_remote_copy(
            src_ref=xr.at[i, s],
            dst_ref=ans.at[k],
            send_sem=a_send,
            recv_sem=a_recv.at[i],
            device_id=(peer_of(h, i, s, -1), me),
            device_id_type=MESH,
        )

    def give_back(i):
        for d in range(1, NX):
            x_copy(i, d).wait_recv()

        @pl.when(i == 0)
        def _():
            ans[0] = xr[0, 0]

        @pl.when(i > 0)
        def _():
            a_copy(i, 0).start()

        for s in range(1, PER):
            a_copy(i, s).start()

    def wait_chunk(buf, sem, i):
        @pl.when(i == 0)
        def _():
            part = buf.at[pl.ds(1, PER - 1)]
            pltpu.make_async_copy(part, part, sem.at[0]).wait()

        @pl.when(i > 0)
        def _():
            part = buf.at[pl.ds(i * PER, PER)]
            pltpu.make_async_copy(part, part, sem.at[i]).wait()

    half_scale = 0.5 * DH ** (-0.5)

    def attend(i, carry):
        wait_chunk(recvm, fm_recv, i)
        wait_chunk(recvq, fq_recv, i)
        for s in range(PER):
            for c in range(CAP):
                mexp[pl.ds((s * CAP + c) * CAND, CAND), :] = jnp.broadcast_to(
                    recvm[i * PER + s, :, c * 64 : c * 64 + 64], (CAND, 64)
                )
        q = recvq[pl.ds(i * PER, PER)].reshape(ROWS, 2 * DH)
        done = []
        for head in range(2):
            lanes = slice(head * DH, (head + 1) * DH)
            qh = q[:, lanes]
            total = None
            for u in range(2):
                for g in range(WIN // GRP):
                    first = u * HBLK + jnp.maximum(hb_ref[u] - WIN, 0) + g * GRP
                    vals = v_v[pl.ds(first, GRP), :, lanes].reshape(GRP * 128, DH)
                    s = jnp.dot(
                        qh,
                        kt[u * 2 + head, :, g * GRP * 128 : (g + 1) * GRP * 128],
                        preferred_element_type=F32,
                    )
                    parts = []
                    for b in range(GRP):
                        lane = u * WIN + g * GRP + b
                        v = s[:, b * 128 : (b + 1) * 128] * half_scale
                        w = (v + v * jnp.tanh(v)) * mexp[:, lane : lane + 1]
                        parts.append(w.astype(BF16))
                    w = jnp.concatenate(parts, axis=1)
                    r = jnp.dot(w, vals, preferred_element_type=F32)
                    total = r if total is None else total + r
            done.append(total.astype(BF16))
        stacked = jnp.concatenate(done, axis=0)
        moved = jnp.dot(perm[...], stacked, preferred_element_type=F32).astype(BF16)
        xs[i] = moved.reshape(NX, PER, CAND, DH)
        for d in (2, 1, 3):
            x_copy(i, d).start()
        xr[i, :, me] = xs[i, me]
        for at, d in ((2, 2), (3, 1), (4, 3)):

            @pl.when(i == at)
            def _(d=d):
                g_copy(d).start()


        @pl.when(i > 0)
        def _():
            give_back(i - 1)

        return carry

    lax.fori_loop(0, CHUNKS, attend, 0)
    give_back(jnp.int32(CHUNKS - 1))

    for d in range(1, NX):
        g_copy(d).wait_recv()
    for load in loads[5:]:
        load.wait()

    for p in range(CHUNKS // 2):
        wait_chunk(ans, a_recv, jnp.int32(2 * p))
        wait_chunk(ans, a_recv, jnp.int32(2 * p + 1))
        got = ans[pl.ds(p * 2 * PER, 2 * PER)]
        rows = jnp.concatenate(
            [got[:, x].reshape(2 * PER * CAND, DH) for x in range(NX)], axis=1
        )
        for head in range(2):
            r = jnp.dot(
                place[head, :, p * 256 : (p + 1) * 256], rows, preferred_element_type=F32
            )
            for x in range(NX):
                lo = (x * 2 + head) * DH
                part = r[:, x * DH : (x + 1) * DH]
                if p:
                    part = part + att[:, lo : lo + DH]
                att[:, lo : lo + DH] = part

    def o_copy(t, d):
        there = lax.rem(me + d, NX)
        part = pl.ds(t * 128, 128)
        return pltpu.make_async_remote_copy(
            src_ref=outs.at[there, part],
            dst_ref=out_ref.at[me, part],
            send_sem=o_send.at[t, d - 1],
            recv_sem=o_recv.at[t, d - 1],
            device_id=(h, there),
            device_id_type=MESH,
        )

    def o_own(t):
        part = pl.ds(t * 128, 128)
        return pltpu.make_async_copy(outs.at[me, part], out_ref.at[me, part], own_sem.at[t])

    for t in range(2):
        part = pl.ds(t * 128, 128)
        full = att[part, :]
        mean = jnp.sum(full, axis=-1, keepdims=True) * (1.0 / 1024)
        var = jnp.sum(full * full, axis=-1, keepdims=True) * (1.0 / 1024) - mean * mean
        rstd = 1.0 / jnp.sqrt(var + 1e-5)
        gated = jnp.concatenate(
            [
                ((att[part, b * 256 : (b + 1) * 256] - mean) * rstd * gr[b, part].astype(F32))
                .astype(BF16)
                for b in range(NX)
            ],
            axis=1,
        )
        for d in (2, 1, 3, 0):
            there = lax.rem(me + d, NX)
            acc = csub[there, part].astype(F32) + jnp.dot(
                gated, wo_v[there], preferred_element_type=F32
            )
            if d:
                outs[there, part] = acc.astype(BF16)
                o_copy(t, d).start()
            else:
                outs[there, part] = acc.astype(BF16)
                o_own(t).start()

    for t in range(2):
        o_own(t).wait()
        for d in range(1, NX):
            o_copy(t, d).wait_recv()

    part = sendq.at[pl.ds(1, NH - 1)]
    pltpu.make_async_copy(part, part, fq_send).wait()
    part = sendm.at[pl.ds(1, NH - 1)]
    pltpu.make_async_copy(part, part, fm_send).wait()
    part = ans.at[pl.ds(1, NH - 1)]
    pltpu.make_async_copy(part, part, a_send).wait()
    for d in range(1, NX):
        part = xs.at[:, 0]
        pltpu.make_async_copy(part, part, x_send.at[d - 1]).wait()
        g_copy(d).wait_send()
    for d in range(1, NX):
        o_copy(0, d).wait_send()
        o_copy(1, d).wait_send()


def on_device(
    candidates,
    w_gate,
    w_query,
    w_out,
    gain,
    key_cache,
    value_cache,
    hist_blocks,
    request_owner,
    request_slot,
    block_offsets,
):
    vmem = pl.BlockSpec(memory_space=pltpu.VMEM)
    smem = pl.BlockSpec(memory_space=pltpu.SMEM)
    anyw = pl.BlockSpec(memory_space=pl.ANY)
    dma = pltpu.SemaphoreType.DMA
    out = pl.pallas_call(
        kernel,
        out_shape=jax.ShapeDtypeStruct((NX, REQ * SUB, 256), BF16),
        in_specs=[smem, vmem, vmem, vmem, vmem] + [anyw] * 6,
        out_specs=anyw,
        scratch_shapes=[
            pltpu.VMEM((1024, 1024), BF16),
            pltpu.VMEM((1024, 256), BF16),
            pltpu.VMEM((1024, 256), BF16),
            pltpu.VMEM((NX, 1024, 256), BF16),
            pltpu.VMEM((2 * HBLK, 128, 256), BF16),
            pltpu.VMEM((2 * HBLK, 128, 256), BF16),
            pltpu.VMEM((1024, 256), BF16),
            pltpu.VMEM((8, 1024), F32),
            pltpu.VMEM((NH, 128), F32),
            pltpu.VMEM((NH, CAP * CAND, 256), BF16),
            pltpu.VMEM((NH, 1, 128), F32),
            pltpu.VMEM((NH, CAP * CAND, 256), BF16),
            pltpu.VMEM((NH, 1, 128), F32),
            pltpu.VMEM((ROWS, 64), F32),
            pltpu.VMEM((CHUNKS, NX, PER, CAND, DH), BF16),
            pltpu.VMEM((CHUNKS, PER, NX, CAND, DH), BF16),
            pltpu.VMEM((NH, NX, CAND, DH), BF16),
            pltpu.VMEM((512, 512), BF16),
            pltpu.VMEM((2, 256, 1024), BF16),
            pltpu.VMEM((NX, 256, 256), BF16),
            pltpu.VMEM((256, 256), BF16),
            pltpu.VMEM((NX, 256, 256), BF16),
            pltpu.VMEM((NX, 256, 256), BF16),
            pltpu.VMEM((256, 1024), F32),
            pltpu.VMEM((NX, 256, 256), BF16),
            pltpu.VMEM((4, DH, WIN * 128), BF16),
            dma((9,)),
            dma,
            dma,
            dma((CHUNKS,)),
            dma((CHUNKS,)),
            dma((3,)),
            dma((3,)),
            dma((3,)),
            dma((CHUNKS, 3)),
            dma,
            dma((CHUNKS,)),
            dma((2, 3)),
            dma((2, 3)),
            pltpu.SemaphoreType.REGULAR,
            dma((2,)),
        ],
        compiler_params=pltpu.CompilerParams(
            collective_id=0, has_side_effects=True, vmem_limit_bytes=56 * 1024 * 1024
        ),
        name="attend_remote",
    )(
        hist_blocks,
        request_owner.reshape(1, REQ),
        request_slot.reshape(1, REQ),
        block_offsets.T,
        gain.reshape(1, 256),
        candidates,
        w_query,
        w_gate,
        w_out,
        key_cache.reshape(2 * HBLK, 128, 256),
        value_cache.reshape(2 * HBLK, 128, 256),
    )
    return out.reshape(NX, REQ, SUB, 256).transpose(1, 0, 2, 3).reshape(REQ * CAND, 256)


def solution(mesh):
    in_specs = (
        P("hist", None),
        P(None, "mp"),
        P(None, "mp"),
        P(),
        P("mp"),
        P("hist", None, "mp"),
        P("hist", None, "mp"),
        P("hist"),
        P("hist", None),
        P("hist"),
        P("hist", None),
    )
    return jax.shard_map(
        on_device, mesh=mesh, in_specs=in_specs, out_specs=P("hist", "mp"), check_vma=False
    )
```

```python
import jax
import jax.numpy as jnp
from jax import lax
from jax.experimental import pallas as pl
from jax.experimental.pallas import tpu as pltpu
from jax.sharding import PartitionSpec as P

MESH = pl.DeviceIdType.MESH
F32 = jnp.float32
BF16 = jnp.bfloat16

NZ, NY, NC = 8, 4, 2
NH = NZ * NY * NC
CHUNKS, PER = 8, 8
NX = 4
CAP = 2
CAND = 16
REQ = 64
DH = 128
WIN = 12
HBLK = 24
SUB = CAND // NX
ROWS = PER * CAP * CAND
GRP = 4
UPFRONT = 8


def peer_of(h, low, dz, sign):
    z, y, c = h >> 3, (h >> 1) & 3, h & 1
    z = (z + sign * dz) & (NZ - 1)
    y = (y + sign * (low >> 1)) & (NY - 1)
    return z * (NY * NC) + y * NC + (c ^ (low & 1))


def silu(v):
    half = v * 0.5
    return half + half * jnp.tanh(half)


def kernel(
    hb_ref,
    own_ref,
    slot_ref,
    off_ref,
    gain_ref,
    cand_hbm,
    wq_hbm,
    wg_hbm,
    wo_hbm,
    k_hbm,
    v_hbm,
    out_ref,
    cand_v,
    wq_v,
    wg_v,
    wo_v,
    k_v,
    v_v,
    q_v,
    tcol,
    mall,
    sendq,
    sendm,
    recvq,
    recvm,
    mexp,
    xs,
    xr,
    ans,
    perm,
    place,
    csub,
    r4,
    gs,
    gr,
    att,
    outs,
    kt,
    load_sem,
    fq_send,
    fm_send,
    fq_recv,
    fm_recv,
    g_send,
    g_recv,
    x_send,
    x_recv,
    a_send,
    a_recv,
    o_send,
    o_recv,
    plane_sem,
    own_sem,
):
    h = lax.axis_index("hist")
    me = lax.axis_index("mp")

    barrier = pltpu.get_barrier_semaphore()

    def greet(sem, low, dz):
        pl.semaphore_signal(
            sem, inc=1, device_id=(peer_of(h, low, dz, 1), me), device_id_type=MESH
        )

    for d in range(1, PER):
        greet(barrier, 0, d)
    for d in range(1, NX):
        pl.semaphore_signal(
            barrier, inc=1, device_id=(h, lax.rem(me + d, NX)), device_id_type=MESH
        )
    for d in range(1, CHUNKS):
        greet(barrier, d, 0)

    loads = [
        pltpu.make_async_copy(cand_hbm, cand_v, load_sem.at[0]),
        pltpu.make_async_copy(wq_hbm, wq_v, load_sem.at[1]),
        pltpu.make_async_copy(wg_hbm, wg_v, load_sem.at[2]),
        pltpu.make_async_copy(k_hbm, k_v, load_sem.at[3]),
        pltpu.make_async_copy(v_hbm, v_v, load_sem.at[4]),
    ] + [
        pltpu.make_async_copy(
            wo_hbm.at[:, pl.ds(b * 256, 256)], wo_v.at[b], load_sem.at[5 + b]
        )
        for b in range(NX)
    ]
    for load in loads[:2]:
        load.start()

    def same_lanes(row, count):
        return jnp.broadcast_to(row, (count, REQ))

    def lanes_dot(a, b):
        return lax.dot_general(a, b, (((1,), (1,)), ((), ())), preferred_element_type=F32)

    def iota(shape, axis):
        return lax.broadcasted_iota(jnp.int32, shape, axis)

    def flag(hit):
        return jnp.where(hit, 1.0, 0.0)

    own = own_ref[...]
    own_f = own.astype(F32)
    eye = flag(iota((REQ, REQ), 0) == iota((REQ, REQ), 1)).astype(BF16)
    own_col = lanes_dot(eye, same_lanes(own_f, REQ).astype(BF16))
    twin = (own_col == same_lanes(own_f, REQ)) & (iota((REQ, REQ), 0) < iota((REQ, REQ), 1))
    rank = jnp.sum(flag(twin), axis=0, keepdims=True)
    low_own, low_h = own & (NY * NC - 1), lax.rem(h, NY * NC)
    dz = ((own >> 3) - lax.div(h, NY * NC) + NZ) & (NZ - 1)
    dy = ((low_own >> 1) - lax.div(low_h, NC) + NY) & (NY - 1)
    dc = (low_own + lax.rem(low_h, NC)) & (NC - 1)
    step = (dy * NC + dc) * PER + dz
    slot = (step * CAP).astype(F32) + rank
    slot_bf = same_lanes(slot, 128).astype(BF16)
    spread = flag(iota((REQ, 1024), 1) >> 4 == iota((REQ, 1024), 0)).astype(BF16)
    tcol[...] = jnp.dot(
        slot_bf[:8], spread, preferred_element_type=F32
    ) * CAND + (iota((8, 1024), 1) & (CAND - 1)).astype(F32)
    lane = slot_ref[...] * WIN + (WIN - 1)
    counts = jnp.zeros((32, REQ), F32)
    for j in range(WIN):
        counts += flag(same_lanes(lane - off_ref[pl.ds(j, 1), :], 32) == iota((32, REQ), 0))
    blank = jnp.zeros((32, REQ), F32)
    both = jnp.zeros((NH, 128), F32)
    for c in range(CAP):
        parts = [blank] * (2 * c) + [counts] + [blank] * (3 - 2 * c)
        mine = (iota((NH, REQ), 0) * CAP + c).astype(F32)
        held = flag(same_lanes(slot, NH) == mine).astype(BF16)
        both += lanes_dot(held, jnp.concatenate(parts, axis=0).astype(BF16))
    mall[...] = both

    loads[0].wait()
    loads[1].wait()
    for load in loads[2:]:
        load.start()

    def project(t, carry):
        rows = pl.ds(pl.multiple_of(t * 256, 256), 256)
        acc = jnp.dot(cand_v[rows, :], wq_v[...], preferred_element_type=F32)
        q_v[rows, :] = silu(acc).astype(BF16)
        return carry

    lax.fori_loop(0, 4, project, 0)

    pl.semaphore_wait(barrier, PER - 1 + CHUNKS - 1 + NX - 1)
    for d in range(1, CHUNKS):
        greet(plane_sem, d, 0)

    def fq_copy(i, dz):
        k = i * PER + dz
        return pltpu.make_async_remote_copy(
            src_ref=sendq.at[k],
            dst_ref=recvq.at[k],
            send_sem=fq_send,
            recv_sem=fq_recv.at[i],
            device_id=(peer_of(h, i, dz, 1), me),
            device_id_type=MESH,
        )

    def fm_copy(i, dz):
        k = i * PER + dz
        return pltpu.make_async_remote_copy(
            src_ref=sendm.at[k],
            dst_ref=recvm.at[k],
            send_sem=fm_send,
            recv_sem=fm_recv.at[i],
            device_id=(peer_of(h, i, dz, 1), me),
            device_id_type=MESH,
        )

    def forward(i, carry):
        row = (iota((ROWS, 1024), 0) + i * ROWS).astype(F32)
        pick = flag(row == jnp.broadcast_to(tcol[pl.ds(0, 1), :], (ROWS, 1024))).astype(BF16)
        got = jnp.dot(pick, q_v[...], preferred_element_type=F32).astype(BF16)
        sendq[pl.ds(i * PER, PER)] = got.reshape(PER, CAP * CAND, 2 * DH)

        def one(dz):
            k = i * PER + dz
            sendm[k] = mall[pl.ds(k, 1), :]
            fm_copy(i, dz).start()
            fq_copy(i, dz).start()

        @pl.when(i == 0)
        def _():
            recvq[0] = sendq[0]
            recvm[0] = mall[pl.ds(0, 1), :]

        @pl.when(i == 1)
        def _():
            pl.semaphore_wait(plane_sem, CHUNKS - 1)

        @pl.when(i > 0)
        def _():
            one(0)

        for dz in range(1, PER):
            one(dz)

        return carry

    lax.fori_loop(0, UPFRONT, forward, 0)

    def g_copy(d):
        there = lax.rem(me + d, NX)
        return pltpu.make_async_remote_copy(
            src_ref=gs.at[there],
            dst_ref=gr.at[me],
            send_sem=g_send.at[d - 1],
            recv_sem=g_recv.at[d - 1],
            device_id=(h, there),
            device_id_type=MESH,
        )

    i, col = iota((256, 256), 0), iota((256, 256), 1)
    r4[...] = flag(col == ((i >> 2) & 15) * 16 + (i >> 6) * 4 + (i & 3)).astype(BF16)

    loads[2].wait()

    def gate(t, carry):
        rows = pl.ds(pl.multiple_of(t * 256, 256), 256)
        part = pl.ds(pl.multiple_of(t * 64, 64), 64)
        acc = jnp.dot(cand_v[rows, :], wg_v[...], preferred_element_type=F32)
        g = (silu(acc) * gain_ref[...]).astype(BF16)
        moved = jnp.dot(r4[...], g, preferred_element_type=F32).astype(BF16)
        gs[:, part, :] = moved.reshape(NX, 64, 256)
        mine = r4[pl.ds(pl.multiple_of(me * 64, 64), 64), :]
        for b in range(NX):
            csub[b, part, :] = jnp.dot(
                mine, cand_v[rows, b * 256 : (b + 1) * 256], preferred_element_type=F32
            ).astype(BF16)
        return carry

    lax.fori_loop(0, 4, gate, 0)
    gr[me] = gs[me]

    def one_hot(t, carry):
        rows = pl.ds(pl.multiple_of(t * 128, 128), 128)
        i = lax.broadcasted_iota(jnp.int32, (128, 512), 0) + t * 128
        col = lax.broadcasted_iota(jnp.int32, (128, 512), 1)
        j, src, head = i >> 7, (i >> 4) & 7, (i >> 3) & 1
        slot, c = (i >> 2) & 1, i & 3
        want = head * 256 + src * 32 + slot * 16 + j * 4 + c
        perm[rows, :] = jnp.where(col == want, 1.0, 0.0).astype(BF16)
        return carry

    lax.fori_loop(0, 4, one_hot, 0)

    i = iota((256, REQ), 0)
    spread = flag(i >> 2 == iota((256, REQ), 1)).astype(BF16)
    want = lanes_dot(spread, slot_bf)
    c = iota((256, 128), 0) & 3
    for t in range(8):
        col = iota((256, 128), 1) + t * 128
        for head in range(2):
            sits = ((col >> 4) * 2 + ((col >> 2) & 1)).astype(F32)
            hit = (sits == want) & ((col & 3) == c) & (((col >> 3) & 1) == head)
            place[head, :, t * 128 : (t + 1) * 128] = flag(hit).astype(BF16)

    loads[3].wait()
    for b in range(WIN):
        for u in range(2):
            first = u * HBLK + jnp.maximum(hb_ref[u] - WIN, 0) + b
            for head in range(2):
                kt[u * 2 + head, :, b * 128 : (b + 1) * 128] = k_v[
                    first, :, head * DH : (head + 1) * DH
                ].T
    loads[4].wait()

    def x_copy(i, d):
        there = lax.rem(me + d, NX)
        return pltpu.make_async_remote_copy(
            src_ref=xs.at[i, there],
            dst_ref=xr.at[i, :, me],
            send_sem=x_send.at[d - 1],
            recv_sem=x_recv.at[i, d - 1],
            device_id=(h, there),
            device_id_type=MESH,
        )

    def a_copy(i, s):
        k = i * PER + s
        return pltpu.make_async_remote_copy(
            src_ref=xr.at[i, s],
            dst_ref=ans.at[k],
            send_sem=a_send,
            recv_sem=a_recv.at[i],
            device_id=(peer_of(h, i, s, -1), me),
            device_id_type=MESH,
        )

    def give_back(i):
        for d in range(1, NX):
            x_copy(i, d).wait_recv()

        @pl.when(i == 0)
        def _():
            ans[0] = xr[0, 0]

        @pl.when(i > 0)
        def _():
            a_copy(i, 0).start()

        for s in range(1, PER):
            a_copy(i, s).start()

    def wait_chunk(buf, sem, i):
        @pl.when(i == 0)
        def _():
            part = buf.at[pl.ds(1, PER - 1)]
            pltpu.make_async_copy(part, part, sem.at[0]).wait()

        @pl.when(i > 0)
        def _():
            part = buf.at[pl.ds(i * PER, PER)]
            pltpu.make_async_copy(part, part, sem.at[i]).wait()

    half_scale = 0.5 * DH ** (-0.5)

    def attend(i, carry):
        wait_chunk(recvm, fm_recv, i)
        wait_chunk(recvq, fq_recv, i)
        for s in range(PER):
            for c in range(CAP):
                mexp[pl.ds((s * CAP + c) * CAND, CAND), :] = jnp.broadcast_to(
                    recvm[i * PER + s, :, c * 64 : c * 64 + 64], (CAND, 64)
                )
        q = recvq[pl.ds(i * PER, PER)].reshape(ROWS, 2 * DH)
        done = []
        for head in range(2):
            lanes = slice(head * DH, (head + 1) * DH)
            qh = q[:, lanes]
            total = None
            for u in range(2):
                for g in range(WIN // GRP):
                    first = u * HBLK + jnp.maximum(hb_ref[u] - WIN, 0) + g * GRP
                    vals = v_v[pl.ds(first, GRP), :, lanes].reshape(GRP * 128, DH)
                    s = jnp.dot(
                        qh,
                        kt[u * 2 + head, :, g * GRP * 128 : (g + 1) * GRP * 128],
                        preferred_element_type=F32,
                    )
                    parts = []
                    for b in range(GRP):
                        lane = u * WIN + g * GRP + b
                        v = s[:, b * 128 : (b + 1) * 128] * half_scale
                        w = (v + v * jnp.tanh(v)) * mexp[:, lane : lane + 1]
                        parts.append(w.astype(BF16))
                    w = jnp.concatenate(parts, axis=1)
                    r = jnp.dot(w, vals, preferred_element_type=F32)
                    total = r if total is None else total + r
            done.append(total.astype(BF16))
        stacked = jnp.concatenate(done, axis=0)
        moved = jnp.dot(perm[...], stacked, preferred_element_type=F32).astype(BF16)
        xs[i] = moved.reshape(NX, PER, CAND, DH)
        for d in (2, 1, 3):
            x_copy(i, d).start()
        xr[i, :, me] = xs[i, me]
        for at, d in ((2, 2), (3, 1), (4, 3)):

            @pl.when(i == at)
            def _(d=d):
                g_copy(d).start()


        @pl.when(i > 0)
        def _():
            give_back(i - 1)

        return carry

    lax.fori_loop(0, CHUNKS, attend, 0)
    give_back(jnp.int32(CHUNKS - 1))

    for d in range(1, NX):
        g_copy(d).wait_recv()
    for load in loads[5:]:
        load.wait()

    for p in range(CHUNKS // 2):
        wait_chunk(ans, a_recv, jnp.int32(2 * p))
        wait_chunk(ans, a_recv, jnp.int32(2 * p + 1))
        got = ans[pl.ds(p * 2 * PER, 2 * PER)]
        rows = jnp.concatenate(
            [got[:, x].reshape(2 * PER * CAND, DH) for x in range(NX)], axis=1
        )
        for head in range(2):
            r = jnp.dot(
                place[head, :, p * 256 : (p + 1) * 256], rows, preferred_element_type=F32
            )
            for x in range(NX):
                lo = (x * 2 + head) * DH
                part = r[:, x * DH : (x + 1) * DH]
                if p:
                    part = part + att[:, lo : lo + DH]
                att[:, lo : lo + DH] = part

    def o_copy(t, d):
        there = lax.rem(me + d, NX)
        part = pl.ds(t * 128, 128)
        return pltpu.make_async_remote_copy(
            src_ref=outs.at[there, part],
            dst_ref=out_ref.at[me, part],
            send_sem=o_send.at[t, d - 1],
            recv_sem=o_recv.at[t, d - 1],
            device_id=(h, there),
            device_id_type=MESH,
        )

    def o_own(t):
        part = pl.ds(t * 128, 128)
        return pltpu.make_async_copy(outs.at[me, part], out_ref.at[me, part], own_sem.at[t])

    for t in range(2):
        part = pl.ds(t * 128, 128)
        full = att[part, :]
        mean = jnp.sum(full, axis=-1, keepdims=True) * (1.0 / 1024)
        var = jnp.sum(full * full, axis=-1, keepdims=True) * (1.0 / 1024) - mean * mean
        rstd = 1.0 / jnp.sqrt(var + 1e-5)
        gated = jnp.concatenate(
            [
                ((att[part, b * 256 : (b + 1) * 256] - mean) * rstd * gr[b, part].astype(F32))
                .astype(BF16)
                for b in range(NX)
            ],
            axis=1,
        )
        for d in (2, 1, 3, 0):
            there = lax.rem(me + d, NX)
            acc = csub[there, part].astype(F32) + jnp.dot(
                gated, wo_v[there], preferred_element_type=F32
            )
            if d:
                outs[there, part] = acc.astype(BF16)
                o_copy(t, d).start()
            else:
                outs[there, part] = acc.astype(BF16)
                o_own(t).start()

    for t in range(2):
        o_own(t).wait()
        for d in range(1, NX):
            o_copy(t, d).wait_recv()

    part = sendq.at[pl.ds(1, NH - 1)]
    pltpu.make_async_copy(part, part, fq_send).wait()
    part = sendm.at[pl.ds(1, NH - 1)]
    pltpu.make_async_copy(part, part, fm_send).wait()
    part = ans.at[pl.ds(1, NH - 1)]
    pltpu.make_async_copy(part, part, a_send).wait()
    for d in range(1, NX):
        part = xs.at[:, 0]
        pltpu.make_async_copy(part, part, x_send.at[d - 1]).wait()
        g_copy(d).wait_send()
    for d in range(1, NX):
        o_copy(0, d).wait_send()
        o_copy(1, d).wait_send()


def interleave(in_ref, out_ref):
    i = lax.broadcasted_iota(jnp.int32, (256, 256), 0)
    col = lax.broadcasted_iota(jnp.int32, (256, 256), 1)
    put = jnp.where(i == ((col >> 2) & 15) * 16 + (col >> 6) * 4 + (col & 3), 1.0, 0.0)
    put = put.astype(BF16)
    for t in range(2):
        rows = in_ref[:, t * 64 : (t + 1) * 64, :].reshape(256, 256)
        out_ref[t * 256 : (t + 1) * 256, :] = jnp.dot(
            put, rows, preferred_element_type=F32
        ).astype(BF16)


def on_device(
    candidates,
    w_gate,
    w_query,
    w_out,
    gain,
    key_cache,
    value_cache,
    hist_blocks,
    request_owner,
    request_slot,
    block_offsets,
):
    vmem = pl.BlockSpec(memory_space=pltpu.VMEM)
    smem = pl.BlockSpec(memory_space=pltpu.SMEM)
    anyw = pl.BlockSpec(memory_space=pl.ANY)
    dma = pltpu.SemaphoreType.DMA
    out = pl.pallas_call(
        kernel,
        out_shape=jax.ShapeDtypeStruct((NX, REQ * SUB, 256), BF16),
        in_specs=[smem, vmem, vmem, vmem, vmem] + [anyw] * 6,
        out_specs=anyw,
        scratch_shapes=[
            pltpu.VMEM((1024, 1024), BF16),
            pltpu.VMEM((1024, 256), BF16),
            pltpu.VMEM((1024, 256), BF16),
            pltpu.VMEM((NX, 1024, 256), BF16),
            pltpu.VMEM((2 * HBLK, 128, 256), BF16),
            pltpu.VMEM((2 * HBLK, 128, 256), BF16),
            pltpu.VMEM((1024, 256), BF16),
            pltpu.VMEM((8, 1024), F32),
            pltpu.VMEM((NH, 128), F32),
            pltpu.VMEM((NH, CAP * CAND, 256), BF16),
            pltpu.VMEM((NH, 1, 128), F32),
            pltpu.VMEM((NH, CAP * CAND, 256), BF16),
            pltpu.VMEM((NH, 1, 128), F32),
            pltpu.VMEM((ROWS, 64), F32),
            pltpu.VMEM((CHUNKS, NX, PER, CAND, DH), BF16),
            pltpu.VMEM((CHUNKS, PER, NX, CAND, DH), BF16),
            pltpu.VMEM((NH, NX, CAND, DH), BF16),
            pltpu.VMEM((512, 512), BF16),
            pltpu.VMEM((2, 256, 1024), BF16),
            pltpu.VMEM((NX, 256, 256), BF16),
            pltpu.VMEM((256, 256), BF16),
            pltpu.VMEM((NX, 256, 256), BF16),
            pltpu.VMEM((NX, 256, 256), BF16),
            pltpu.VMEM((256, 1024), F32),
            pltpu.VMEM((NX, 256, 256), BF16),
            pltpu.VMEM((4, DH, WIN * 128), BF16),
            dma((9,)),
            dma,
            dma,
            dma((CHUNKS,)),
            dma((CHUNKS,)),
            dma((3,)),
            dma((3,)),
            dma((3,)),
            dma((CHUNKS, 3)),
            dma,
            dma((CHUNKS,)),
            dma((2, 3)),
            dma((2, 3)),
            pltpu.SemaphoreType.REGULAR,
            dma((2,)),
        ],
        compiler_params=pltpu.CompilerParams(
            collective_id=0, has_side_effects=True, vmem_limit_bytes=56 * 1024 * 1024
        ),
        name="attend_remote",
    )(
        hist_blocks,
        request_owner.reshape(1, REQ),
        request_slot.reshape(1, REQ),
        block_offsets.T,
        gain.reshape(1, 256),
        candidates,
        w_query,
        w_gate,
        w_out,
        key_cache.reshape(2 * HBLK, 128, 256),
        value_cache.reshape(2 * HBLK, 128, 256),
    )
    return pl.pallas_call(
        interleave,
        out_shape=jax.ShapeDtypeStruct((REQ * CAND, 256), BF16),
        grid=(2,),
        in_specs=[pl.BlockSpec((NX, 128, 256), lambda t: (0, t, 0))],
        out_specs=pl.BlockSpec((512, 256), lambda t: (t, 0)),
        name="interleave_rows",
    )(out)


def solution(mesh):
    in_specs = (
        P("hist", None),
        P(None, "mp"),
        P(None, "mp"),
        P(),
        P("mp"),
        P("hist", None, "mp"),
        P("hist", None, "mp"),
        P("hist"),
        P("hist", None),
        P("hist"),
        P("hist", None),
    )
    return jax.shard_map(
        on_device, mesh=mesh, in_specs=in_specs, out_specs=P("hist", "mp"), check_vma=False
    )
```

```python
import jax
import jax.numpy as jnp
from jax import lax
from jax.experimental import pallas as pl
from jax.experimental.pallas import tpu as pltpu
from jax.sharding import PartitionSpec as P

MESH = pl.DeviceIdType.MESH
F32 = jnp.float32
BF16 = jnp.bfloat16

NZ, NY, NC = 8, 4, 2
NH = NZ * NY * NC
CHUNKS, PER = 8, 8
NX = 4
CAP = 2
CAND = 16
REQ = 64
DH = 128
WIN = 12
HBLK = 24
SUB = CAND // NX
ROWS = PER * CAP * CAND
GRP = 4
UPFRONT = 8
BLOCKS = 4
BROWS = 64


def peer_of(h, low, dz, sign):
    z, y, c = h >> 3, (h >> 1) & 3, h & 1
    z = (z + sign * dz) & (NZ - 1)
    y = (y + sign * (low >> 1)) & (NY - 1)
    return z * (NY * NC) + y * NC + (c ^ (low & 1))


def silu(v):
    half = v * 0.5
    return half + half * jnp.tanh(half)


def kernel(
    hb_ref,
    own_ref,
    slot_ref,
    off_ref,
    gain_ref,
    cand_hbm,
    wq_hbm,
    wg_hbm,
    wo_hbm,
    k_hbm,
    v_hbm,
    out_ref,
    cand_v,
    wq_v,
    wg_v,
    wo_v,
    k_v,
    v_v,
    q_v,
    tcol,
    mall,
    sendq,
    sendm,
    recvq,
    recvm,
    mexp,
    xs,
    xr,
    ans,
    perm,
    place,
    csub,
    r4,
    gs,
    gr,
    att,
    outs,
    kt,
    load_sem,
    fq_send,
    fm_send,
    fq_recv,
    fm_recv,
    g_send,
    g_recv,
    x_send,
    x_recv,
    a_send,
    a_recv,
    o_send,
    o_recv,
    plane_sem,
    own_sem,
):
    h = lax.axis_index("hist")
    me = lax.axis_index("mp")

    barrier = pltpu.get_barrier_semaphore()

    def greet(sem, low, dz):
        pl.semaphore_signal(
            sem, inc=1, device_id=(peer_of(h, low, dz, 1), me), device_id_type=MESH
        )

    for d in range(1, PER):
        greet(barrier, 0, d)
    for d in range(1, NX):
        pl.semaphore_signal(
            barrier, inc=1, device_id=(h, lax.rem(me + d, NX)), device_id_type=MESH
        )
    for d in range(1, CHUNKS):
        greet(barrier, d, 0)

    loads = [
        pltpu.make_async_copy(cand_hbm, cand_v, load_sem.at[0]),
        pltpu.make_async_copy(wq_hbm, wq_v, load_sem.at[1]),
        pltpu.make_async_copy(wg_hbm, wg_v, load_sem.at[2]),
        pltpu.make_async_copy(k_hbm, k_v, load_sem.at[3]),
        pltpu.make_async_copy(v_hbm, v_v, load_sem.at[4]),
    ] + [
        pltpu.make_async_copy(
            wo_hbm.at[:, pl.ds(b * 256, 256)], wo_v.at[b], load_sem.at[5 + b]
        )
        for b in range(NX)
    ]
    for load in loads[:2]:
        load.start()

    def same_lanes(row, count):
        return jnp.broadcast_to(row, (count, REQ))

    def lanes_dot(a, b):
        return lax.dot_general(a, b, (((1,), (1,)), ((), ())), preferred_element_type=F32)

    def iota(shape, axis):
        return lax.broadcasted_iota(jnp.int32, shape, axis)

    def flag(hit):
        return jnp.where(hit, 1.0, 0.0)

    own = own_ref[...]
    own_f = own.astype(F32)
    eye = flag(iota((REQ, REQ), 0) == iota((REQ, REQ), 1)).astype(BF16)
    own_col = lanes_dot(eye, same_lanes(own_f, REQ).astype(BF16))
    twin = (own_col == same_lanes(own_f, REQ)) & (iota((REQ, REQ), 0) < iota((REQ, REQ), 1))
    rank = jnp.sum(flag(twin), axis=0, keepdims=True)
    low_own, low_h = own & (NY * NC - 1), lax.rem(h, NY * NC)
    dz = ((own >> 3) - lax.div(h, NY * NC) + NZ) & (NZ - 1)
    dy = ((low_own >> 1) - lax.div(low_h, NC) + NY) & (NY - 1)
    dc = (low_own + lax.rem(low_h, NC)) & (NC - 1)
    step = (dy * NC + dc) * PER + dz
    slot = (step * CAP).astype(F32) + rank
    slot_bf = same_lanes(slot, 128).astype(BF16)
    spread = flag(iota((REQ, 1024), 1) >> 4 == iota((REQ, 1024), 0)).astype(BF16)
    tcol[...] = jnp.dot(
        slot_bf[:8], spread, preferred_element_type=F32
    ) * CAND + (iota((8, 1024), 1) & (CAND - 1)).astype(F32)
    lane = slot_ref[...] * WIN + (WIN - 1)
    counts = jnp.zeros((32, REQ), F32)
    for j in range(WIN):
        counts += flag(same_lanes(lane - off_ref[pl.ds(j, 1), :], 32) == iota((32, REQ), 0))
    blank = jnp.zeros((32, REQ), F32)
    both = jnp.zeros((NH, 128), F32)
    for c in range(CAP):
        parts = [blank] * (2 * c) + [counts] + [blank] * (3 - 2 * c)
        mine = (iota((NH, REQ), 0) * CAP + c).astype(F32)
        held = flag(same_lanes(slot, NH) == mine).astype(BF16)
        both += lanes_dot(held, jnp.concatenate(parts, axis=0).astype(BF16))
    mall[...] = both

    loads[0].wait()
    loads[1].wait()
    for load in loads[2:]:
        load.start()

    def project(t, carry):
        rows = pl.ds(pl.multiple_of(t * 256, 256), 256)
        acc = jnp.dot(cand_v[rows, :], wq_v[...], preferred_element_type=F32)
        q_v[rows, :] = silu(acc).astype(BF16)
        return carry

    lax.fori_loop(0, 4, project, 0)

    pl.semaphore_wait(barrier, PER - 1 + CHUNKS - 1 + NX - 1)
    for d in range(1, CHUNKS):
        greet(plane_sem, d, 0)

    def fq_copy(i, dz):
        k = i * PER + dz
        return pltpu.make_async_remote_copy(
            src_ref=sendq.at[k],
            dst_ref=recvq.at[k],
            send_sem=fq_send,
            recv_sem=fq_recv.at[i],
            device_id=(peer_of(h, i, dz, 1), me),
            device_id_type=MESH,
        )

    def fm_copy(i, dz):
        k = i * PER + dz
        return pltpu.make_async_remote_copy(
            src_ref=sendm.at[k],
            dst_ref=recvm.at[k],
            send_sem=fm_send,
            recv_sem=fm_recv.at[i],
            device_id=(peer_of(h, i, dz, 1), me),
            device_id_type=MESH,
        )

    def forward(i, carry):
        row = (iota((ROWS, 1024), 0) + i * ROWS).astype(F32)
        pick = flag(row == jnp.broadcast_to(tcol[pl.ds(0, 1), :], (ROWS, 1024))).astype(BF16)
        got = jnp.dot(pick, q_v[...], preferred_element_type=F32).astype(BF16)
        sendq[pl.ds(i * PER, PER)] = got.reshape(PER, CAP * CAND, 2 * DH)

        def one(dz):
            k = i * PER + dz
            sendm[k] = mall[pl.ds(k, 1), :]
            fm_copy(i, dz).start()
            fq_copy(i, dz).start()

        @pl.when(i == 0)
        def _():
            recvq[0] = sendq[0]
            recvm[0] = mall[pl.ds(0, 1), :]

        @pl.when(i == 1)
        def _():
            pl.semaphore_wait(plane_sem, CHUNKS - 1)

        @pl.when(i > 0)
        def _():
            one(0)

        for dz in range(1, PER):
            one(dz)

        return carry

    lax.fori_loop(0, UPFRONT, forward, 0)

    def g_copy(d):
        there = lax.rem(me + d, NX)
        return pltpu.make_async_remote_copy(
            src_ref=gs.at[there],
            dst_ref=gr.at[me],
            send_sem=g_send.at[d - 1],
            recv_sem=g_recv.at[d - 1],
            device_id=(h, there),
            device_id_type=MESH,
        )

    i, col = iota((256, 256), 0), iota((256, 256), 1)
    r4[...] = flag(col == ((i >> 2) & 15) * 16 + (i >> 6) * 4 + (i & 3)).astype(BF16)

    loads[2].wait()

    def gate(t, carry):
        rows = pl.ds(pl.multiple_of(t * 256, 256), 256)
        part = pl.ds(pl.multiple_of(t * 64, 64), 64)
        acc = jnp.dot(cand_v[rows, :], wg_v[...], preferred_element_type=F32)
        g = (silu(acc) * gain_ref[...]).astype(BF16)
        moved = jnp.dot(r4[...], g, preferred_element_type=F32).astype(BF16)
        gs[:, part, :] = moved.reshape(NX, 64, 256)
        mine = r4[pl.ds(pl.multiple_of(me * 64, 64), 64), :]
        for b in range(NX):
            csub[b, part, :] = jnp.dot(
                mine, cand_v[rows, b * 256 : (b + 1) * 256], preferred_element_type=F32
            ).astype(BF16)
        return carry

    lax.fori_loop(0, 4, gate, 0)
    gr[me] = gs[me]

    def one_hot(t, carry):
        rows = pl.ds(pl.multiple_of(t * 128, 128), 128)
        i = lax.broadcasted_iota(jnp.int32, (128, 512), 0) + t * 128
        col = lax.broadcasted_iota(jnp.int32, (128, 512), 1)
        j, src, head = i >> 7, (i >> 4) & 7, (i >> 3) & 1
        slot, c = (i >> 2) & 1, i & 3
        want = head * 256 + src * 32 + slot * 16 + j * 4 + c
        perm[rows, :] = jnp.where(col == want, 1.0, 0.0).astype(BF16)
        return carry

    lax.fori_loop(0, 4, one_hot, 0)

    i = iota((256, REQ), 0)
    spread = flag(i >> 2 == iota((256, REQ), 1)).astype(BF16)
    want = lanes_dot(spread, slot_bf)
    c = iota((256, 128), 0) & 3
    for t in range(8):
        col = iota((256, 128), 1) + t * 128
        for head in range(2):
            sits = ((col >> 4) * 2 + ((col >> 2) & 1)).astype(F32)
            hit = (sits == want) & ((col & 3) == c) & (((col >> 3) & 1) == head)
            place[head, :, t * 128 : (t + 1) * 128] = flag(hit).astype(BF16)

    loads[3].wait()
    for b in range(WIN):
        for u in range(2):
            first = u * HBLK + jnp.maximum(hb_ref[u] - WIN, 0) + b
            for head in range(2):
                kt[u * 2 + head, :, b * 128 : (b + 1) * 128] = k_v[
                    first, :, head * DH : (head + 1) * DH
                ].T
    loads[4].wait()

    def x_copy(i, d):
        there = lax.rem(me + d, NX)
        return pltpu.make_async_remote_copy(
            src_ref=xs.at[i, there],
            dst_ref=xr.at[i, :, me],
            send_sem=x_send.at[d - 1],
            recv_sem=x_recv.at[i, d - 1],
            device_id=(h, there),
            device_id_type=MESH,
        )

    def a_copy(i, s):
        k = i * PER + s
        return pltpu.make_async_remote_copy(
            src_ref=xr.at[i, s],
            dst_ref=ans.at[k],
            send_sem=a_send,
            recv_sem=a_recv.at[i],
            device_id=(peer_of(h, i, s, -1), me),
            device_id_type=MESH,
        )

    def give_back(i):
        for d in range(1, NX):
            x_copy(i, d).wait_recv()

        @pl.when(i == 0)
        def _():
            ans[0] = xr[0, 0]

        @pl.when(i > 0)
        def _():
            a_copy(i, 0).start()

        for s in range(1, PER):
            a_copy(i, s).start()

    def wait_chunk(buf, sem, i):
        @pl.when(i == 0)
        def _():
            part = buf.at[pl.ds(1, PER - 1)]
            pltpu.make_async_copy(part, part, sem.at[0]).wait()

        @pl.when(i > 0)
        def _():
            part = buf.at[pl.ds(i * PER, PER)]
            pltpu.make_async_copy(part, part, sem.at[i]).wait()

    half_scale = 0.5 * DH ** (-0.5)

    def attend(i, carry):
        wait_chunk(recvm, fm_recv, i)
        wait_chunk(recvq, fq_recv, i)
        for s in range(PER):
            for c in range(CAP):
                mexp[pl.ds((s * CAP + c) * CAND, CAND), :] = jnp.broadcast_to(
                    recvm[i * PER + s, :, c * 64 : c * 64 + 64], (CAND, 64)
                )
        q = recvq[pl.ds(i * PER, PER)].reshape(ROWS, 2 * DH)
        done = []
        for head in range(2):
            lanes = slice(head * DH, (head + 1) * DH)
            qh = q[:, lanes]
            total = None
            for u in range(2):
                for g in range(WIN // GRP):
                    first = u * HBLK + jnp.maximum(hb_ref[u] - WIN, 0) + g * GRP
                    vals = v_v[pl.ds(first, GRP), :, lanes].reshape(GRP * 128, DH)
                    s = jnp.dot(
                        qh,
                        kt[u * 2 + head, :, g * GRP * 128 : (g + 1) * GRP * 128],
                        preferred_element_type=F32,
                    )
                    parts = []
                    for b in range(GRP):
                        lane = u * WIN + g * GRP + b
                        v = s[:, b * 128 : (b + 1) * 128] * half_scale
                        w = (v + v * jnp.tanh(v)) * mexp[:, lane : lane + 1]
                        parts.append(w.astype(BF16))
                    w = jnp.concatenate(parts, axis=1)
                    r = jnp.dot(w, vals, preferred_element_type=F32)
                    total = r if total is None else total + r
            done.append(total.astype(BF16))
        stacked = jnp.concatenate(done, axis=0)
        moved = jnp.dot(perm[...], stacked, preferred_element_type=F32).astype(BF16)
        xs[i] = moved.reshape(NX, PER, CAND, DH)
        for d in (2, 1, 3):
            x_copy(i, d).start()
        xr[i, :, me] = xs[i, me]
        for at, d in ((2, 2), (3, 1), (4, 3)):

            @pl.when(i == at)
            def _(d=d):
                g_copy(d).start()


        @pl.when(i > 0)
        def _():
            give_back(i - 1)

        return carry

    lax.fori_loop(0, CHUNKS, attend, 0)
    give_back(jnp.int32(CHUNKS - 1))

    for d in range(1, NX):
        g_copy(d).wait_recv()
    for load in loads[5:]:
        load.wait()

    for p in range(CHUNKS // 2):
        wait_chunk(ans, a_recv, jnp.int32(2 * p))
        wait_chunk(ans, a_recv, jnp.int32(2 * p + 1))
        got = ans[pl.ds(p * 2 * PER, 2 * PER)]
        rows = jnp.concatenate(
            [got[:, x].reshape(2 * PER * CAND, DH) for x in range(NX)], axis=1
        )
        for head in range(2):
            r = jnp.dot(
                place[head, :, p * 256 : (p + 1) * 256], rows, preferred_element_type=F32
            )
            for x in range(NX):
                lo = (x * 2 + head) * DH
                part = r[:, x * DH : (x + 1) * DH]
                if p:
                    part = part + att[:, lo : lo + DH]
                att[:, lo : lo + DH] = part

    def o_copy(t, d):
        there = lax.rem(me + d, NX)
        part = pl.ds(t * BROWS, BROWS)
        return pltpu.make_async_remote_copy(
            src_ref=outs.at[there, part],
            dst_ref=out_ref.at[me, part],
            send_sem=o_send.at[t, d - 1],
            recv_sem=o_recv.at[t, d - 1],
            device_id=(h, there),
            device_id_type=MESH,
        )

    def o_own(t):
        part = pl.ds(t * BROWS, BROWS)
        return pltpu.make_async_copy(outs.at[me, part], out_ref.at[me, part], own_sem.at[t])

    kept = []
    for t in range(BLOCKS):
        part = pl.ds(t * BROWS, BROWS)
        full = att[part, :]
        mean = jnp.sum(full, axis=-1, keepdims=True) * (1.0 / 1024)
        var = jnp.sum(full * full, axis=-1, keepdims=True) * (1.0 / 1024) - mean * mean
        rstd = 1.0 / jnp.sqrt(var + 1e-5)
        gated = jnp.concatenate(
            [
                ((att[part, b * 256 : (b + 1) * 256] - mean) * rstd * gr[b, part].astype(F32))
                .astype(BF16)
                for b in range(NX)
            ],
            axis=1,
        )
        for d in (2, 1, 3):
            there = lax.rem(me + d, NX)
            acc = csub[there, part].astype(F32) + jnp.dot(
                gated, wo_v[there], preferred_element_type=F32
            )
            outs[there, part] = acc.astype(BF16)
            o_copy(t, d).start()
        kept.append(gated)
    for t in range(BLOCKS):
        part = pl.ds(t * BROWS, BROWS)
        acc = csub[me, part].astype(F32) + jnp.dot(
            kept[t], wo_v[me], preferred_element_type=F32
        )
        outs[me, part] = acc.astype(BF16)
        o_own(t).start()

    for t in range(BLOCKS):
        o_own(t).wait()
        for d in range(1, NX):
            o_copy(t, d).wait_recv()

    part = sendq.at[pl.ds(1, NH - 1)]
    pltpu.make_async_copy(part, part, fq_send).wait()
    part = sendm.at[pl.ds(1, NH - 1)]
    pltpu.make_async_copy(part, part, fm_send).wait()
    part = ans.at[pl.ds(1, NH - 1)]
    pltpu.make_async_copy(part, part, a_send).wait()
    for d in range(1, NX):
        part = xs.at[:, 0]
        pltpu.make_async_copy(part, part, x_send.at[d - 1]).wait()
        g_copy(d).wait_send()
    for d in range(1, NX):
        for t in range(BLOCKS):
            o_copy(t, d).wait_send()


def interleave(in_ref, out_ref):
    i = lax.broadcasted_iota(jnp.int32, (256, 256), 0)
    col = lax.broadcasted_iota(jnp.int32, (256, 256), 1)
    put = jnp.where(i == ((col >> 2) & 15) * 16 + (col >> 6) * 4 + (col & 3), 1.0, 0.0)
    put = put.astype(BF16)
    for t in range(2):
        rows = in_ref[:, t * 64 : (t + 1) * 64, :].reshape(256, 256)
        out_ref[t * 256 : (t + 1) * 256, :] = jnp.dot(
            put, rows, preferred_element_type=F32
        ).astype(BF16)


def on_device(
    candidates,
    w_gate,
    w_query,
    w_out,
    gain,
    key_cache,
    value_cache,
    hist_blocks,
    request_owner,
    request_slot,
    block_offsets,
):
    vmem = pl.BlockSpec(memory_space=pltpu.VMEM)
    smem = pl.BlockSpec(memory_space=pltpu.SMEM)
    anyw = pl.BlockSpec(memory_space=pl.ANY)
    dma = pltpu.SemaphoreType.DMA
    out = pl.pallas_call(
        kernel,
        out_shape=jax.ShapeDtypeStruct((NX, REQ * SUB, 256), BF16),
        in_specs=[smem, vmem, vmem, vmem, vmem] + [anyw] * 6,
        out_specs=anyw,
        scratch_shapes=[
            pltpu.VMEM((1024, 1024), BF16),
            pltpu.VMEM((1024, 256), BF16),
            pltpu.VMEM((1024, 256), BF16),
            pltpu.VMEM((NX, 1024, 256), BF16),
            pltpu.VMEM((2 * HBLK, 128, 256), BF16),
            pltpu.VMEM((2 * HBLK, 128, 256), BF16),
            pltpu.VMEM((1024, 256), BF16),
            pltpu.VMEM((8, 1024), F32),
            pltpu.VMEM((NH, 128), F32),
            pltpu.VMEM((NH, CAP * CAND, 256), BF16),
            pltpu.VMEM((NH, 1, 128), F32),
            pltpu.VMEM((NH, CAP * CAND, 256), BF16),
            pltpu.VMEM((NH, 1, 128), F32),
            pltpu.VMEM((ROWS, 64), F32),
            pltpu.VMEM((CHUNKS, NX, PER, CAND, DH), BF16),
            pltpu.VMEM((CHUNKS, PER, NX, CAND, DH), BF16),
            pltpu.VMEM((NH, NX, CAND, DH), BF16),
            pltpu.VMEM((512, 512), BF16),
            pltpu.VMEM((2, 256, 1024), BF16),
            pltpu.VMEM((NX, 256, 256), BF16),
            pltpu.VMEM((256, 256), BF16),
            pltpu.VMEM((NX, 256, 256), BF16),
            pltpu.VMEM((NX, 256, 256), BF16),
            pltpu.VMEM((256, 1024), F32),
            pltpu.VMEM((NX, 256, 256), BF16),
            pltpu.VMEM((4, DH, WIN * 128), BF16),
            dma((9,)),
            dma,
            dma,
            dma((CHUNKS,)),
            dma((CHUNKS,)),
            dma((3,)),
            dma((3,)),
            dma((3,)),
            dma((CHUNKS, 3)),
            dma,
            dma((CHUNKS,)),
            dma((BLOCKS, 3)),
            dma((BLOCKS, 3)),
            pltpu.SemaphoreType.REGULAR,
            dma((BLOCKS,)),
        ],
        compiler_params=pltpu.CompilerParams(
            collective_id=0, has_side_effects=True, vmem_limit_bytes=56 * 1024 * 1024
        ),
        name="attend_remote",
    )(
        hist_blocks,
        request_owner.reshape(1, REQ),
        request_slot.reshape(1, REQ),
        block_offsets.T,
        gain.reshape(1, 256),
        candidates,
        w_query,
        w_gate,
        w_out,
        key_cache.reshape(2 * HBLK, 128, 256),
        value_cache.reshape(2 * HBLK, 128, 256),
    )
    return pl.pallas_call(
        interleave,
        out_shape=jax.ShapeDtypeStruct((REQ * CAND, 256), BF16),
        grid=(2,),
        in_specs=[pl.BlockSpec((NX, 128, 256), lambda t: (0, t, 0))],
        out_specs=pl.BlockSpec((512, 256), lambda t: (t, 0)),
        name="interleave_rows",
    )(out)


def solution(mesh):
    in_specs = (
        P("hist", None),
        P(None, "mp"),
        P(None, "mp"),
        P(),
        P("mp"),
        P("hist", None, "mp"),
        P("hist", None, "mp"),
        P("hist"),
        P("hist", None),
        P("hist"),
        P("hist", None),
    )
    return jax.shard_map(
        on_device, mesh=mesh, in_specs=in_specs, out_specs=P("hist", "mp"), check_vma=False
    )
```
